32 devices in a mesh: parts: 2 (over y), latent: 4 (over z), dp: 4 (over x, core).
Axes of the slice: x: 2, y: 2, z: 4, core: 2. Of those that a mesh axis runs over, the one named last changes fastest.
Arguments:
- tokens: bfloat16 [8192, 3072], P(('parts', 'latent'), 'dp'), parts along dimension 0, may hold values from -6 to 6
- target: bfloat16 [8192, 3072], P(('parts', 'latent'), 'dp'), parts along dimension 0, may hold values from -6 to 6
- enc_weight: bfloat16 [6144, 4096], P(('parts', 'dp'), 'latent'), parts along dimension 0, may hold values from -0.109375 to 0.109375
- dec_weight: bfloat16 [8192, 3072], P(('parts', 'latent'), 'dp'), parts along dimension 0, may hold values from -0.5 to 0.5
- enc_bias: float32 [8192], P(('parts', 'latent')), parts along dimension 0, may hold values from -3 to 3
- dec_bias: float32 [6144], P(('parts', 'dp')), parts along dimension 0, may hold values from -3 to 3
- active: int32 [64, 8], P(('parts', 'latent')), parts along dimension 0, may hold values from 0 to 31, as said below
- counts: int32 [64], P(('parts', 'latent')), parts along dimension 0, may hold values from 0 to 8, as said below
Outputs:
- grad_enc: bfloat16 [6144, 4096], P(('parts', 'dp'), 'latent'), parts along dimension 0
- grad_dec: bfloat16 [8192, 3072], P(('parts', 'latent'), 'dp'), parts along dimension 0
The draws below stay inside these ranges and needn't reach their ends.
There are 2 independent parts, one for each index of `parts`. The reference program is written for one: setup_inputs(seed, part) draws one part's arguments, and reference() takes and returns one part's arrays. A program takes and returns all parts, laid end to end along the dimension named above; each array names one. Nothing has to cross between parts.
Inputs may be any that keep to these rules, and one draw needn't show every extreme that they name: The first counts[t] entries of row t are distinct latent block ids, the blocks active for token block t; later entries are arbitrary ids. Of the 8 token blocks of one latent index, at most one has active blocks held by any one latent index. A token block has at most 2 active blocks held by one latent index, and this is reached. All token blocks together have at most 6 pairs whose block one latent index holds, and this is reached. counts[t] is how many leading entries of row t of active are used; some token block uses all 8 entries.
All inputs are finite; a program needn't handle non-finite values.
Results may differ from the reference program's by a relative error of at most 0.018.
Values may be sent and summed in bfloat16 or wider, within the bound.
A program may use at most 128 MiB of HBM per device.

```python
import jax
import jax.numpy as jnp
from jax import lax

BLK = 128
D = 3072
OWN_BLOCKS = 8
MB = 2
TBD = 8
F = 4096
NBLK = 32
TOKENS = 4096
N_LATENT = 4
N_DP = 4


def lay_out(key):
    load_key, star_key, order_key, depth_key, block_key, place_key = jax.random.split(key, 6)
    full_key = jax.random.fold_in(key, 5)
    coin_key = jax.random.fold_in(key, 6)
    owners = N_LATENT
    most_sources = N_LATENT * 3 // 4
    least_sources = max(1, N_LATENT // 4)
    owner_ids = jnp.arange(owners, dtype=jnp.int32)
    busiest_owner = jax.random.randint(star_key, (), 0, owners)
    full_source = jax.random.randint(full_key, (), 0, owners)
    is_full = (owner_ids == full_source)[None, :]
    owner_load = jax.random.randint(load_key, (owners,), least_sources, most_sources + 1)
    owner_load = jnp.where(owner_ids == busiest_owner, most_sources, owner_load)
    order_scores = jax.random.randint(order_key, (owners, owners), 0, 1 << 20) * owners + owner_ids[None, :]
    order_scores = jnp.where(is_full, -1, order_scores)
    ranking = jnp.argsort(jnp.argsort(order_scores, axis=1), axis=1)
    chosen = ranking < owner_load[:, None]
    block_depth = jax.random.randint(depth_key, (owners, owners), 1, MB + 1)
    coin = jax.random.randint(coin_key, (owners, owners), 0, 4)
    block_depth = jnp.where(coin < 3, MB, block_depth)
    block_depth = jnp.where((owner_ids == busiest_owner)[:, None], MB, block_depth)
    block_depth = jnp.where(is_full, MB, block_depth)
    target_block = jax.random.randint(block_key, (owners, owners), 0, TBD)
    target_block = jnp.where(is_full, 0, target_block)
    place_scores = jax.random.randint(place_key, (owners, owners, OWN_BLOCKS), 0, 1 << 20) * OWN_BLOCKS + jnp.arange(OWN_BLOCKS, dtype=jnp.int32)
    places = jnp.argsort(place_scores, axis=2)[:, :, :MB]
    slot_ids = jnp.arange(MB, dtype=jnp.int32)
    block_ids = owner_ids[:, None, None] * OWN_BLOCKS + places
    kept_pairs = chosen[:, :, None] & (slot_ids[None, None, :] < block_depth[:, :, None])
    columns = jnp.arange(TBD, dtype=jnp.int32)
    present = kept_pairs[:, :, None, :] & (target_block[:, :, None, None] == columns[None, None, :, None])
    all_ids = jnp.broadcast_to(block_ids[:, :, None, :], present.shape)
    present = jnp.transpose(present, (1, 2, 0, 3)).reshape(N_LATENT * TBD, N_LATENT * MB)
    all_ids = jnp.transpose(all_ids, (1, 2, 0, 3)).reshape(N_LATENT * TBD, N_LATENT * MB)
    sort_key = (1 - present.astype(jnp.int32)) * (N_LATENT * MB) + jnp.arange(N_LATENT * MB, dtype=jnp.int32)[None, :]
    ordering = jnp.argsort(sort_key, axis=1)
    packed = jnp.take_along_axis(all_ids, ordering, axis=1)
    used_count = jnp.sum(present.astype(jnp.int32), axis=1)
    return (packed, used_count)


def draw_active(key, part):
    packed, used_count = lay_out(key)
    key = jax.random.fold_in(key, 7)
    filler = jax.random.randint(key, packed.shape, 0, NBLK)
    position = jnp.arange(packed.shape[1], dtype=jnp.int32)[None, :]
    return jnp.where(position < used_count[:, None], packed, filler).astype(jnp.int32)


def draw_counts(key, part):
    packed, used_count = lay_out(key)
    return used_count.astype(jnp.int32)


def block_scale(key, dims, cuts, low, high):
    loudness = 1.0
    for axis_at, shards_of in cuts:
        heights = jax.random.uniform(jax.random.fold_in(jax.random.fold_in(key, 6), axis_at), (shards_of,), jnp.float32, low / len(cuts), high / len(cuts))
        loudness = loudness * jnp.repeat(jnp.exp(heights), dims[axis_at] // shards_of).reshape((-1,) + (1,) * (len(dims) - 1 - axis_at))
    return loudness


def centred(own_key, extent, deviation, most, pieces=(), kind=jnp.bfloat16):
    result = deviation * jax.random.normal(own_key, extent, jnp.float32)
    if pieces:
        result = result * block_scale(own_key, extent, pieces, -0.22, 0.18)
    return jnp.clip(result, -most, most).astype(kind)


def setup_inputs(seed: int = 0, part: int = 0) -> dict:
    streams_of = jax.random.split(jax.random.key(seed), 9)
    part_splits = jax.random.split(jax.random.fold_in(streams_of[8], part), 9)
    return {
        "tokens": centred(part_splits[0], (TOKENS, D), 1.0, 6.0, ((0, 4), (1, 4))),
        "target": centred(part_splits[1], (TOKENS, D), 1.0, 6.0, ((0, 4), (1, 4))),
        "enc_weight": centred(part_splits[2], (D, F), D ** -0.5, 0.109375, ((0, 4), (1, 4))),
        "dec_weight": centred(part_splits[3], (F, D), BLK ** -0.5, 0.5, ((0, 4), (1, 4))),
        "enc_bias": centred(part_splits[4], (F,), 0.5, 3.0, ((0, 4),), jnp.float32),
        "dec_bias": centred(part_splits[5], (D,), 0.5, 3.0, ((0, 4),), jnp.float32),
        "active": draw_active(jax.random.fold_in(jax.random.fold_in(streams_of[8], part), 71), part),
        "counts": draw_counts(jax.random.fold_in(jax.random.fold_in(streams_of[8], part), 71), part),
    }


def gelu_back(pre_sum, upstream):
    ignored, pullback = jax.vjp(lambda values: jax.nn.gelu(values, approximate=True), pre_sum)
    return pullback(upstream)[0]

def reference(tokens, target, enc_weight, dec_weight, enc_bias, dec_bias, active, counts):
    block_count = counts.shape[0]
    features = tokens.shape[1]
    group_width = features // N_DP
    list_pos = jnp.arange(active.shape[1], dtype=jnp.int32)
    live_entry = list_pos[None, :] < counts[:, None]
    block_ids = jnp.arange(NBLK, dtype=jnp.int32)
    member = jnp.any(live_entry[:, :, None] & (active[:, :, None] == block_ids[None, None, :]), axis=1)
    member = member.reshape(block_count, N_LATENT, OWN_BLOCKS).astype(jnp.int32)
    before = jnp.cumsum(member, axis=2) - member
    slot_ids = jnp.arange(MB, dtype=jnp.int32)
    place_ids = jnp.arange(OWN_BLOCKS, dtype=jnp.int32)
    matches = (member[:, :, None, :] == 1) & (before[:, :, None, :] == slot_ids[None, None, :, None])
    pair_place = lax.optimization_barrier(jnp.sum(jnp.where(matches, place_ids[None, None, None, :], 0), axis=3)).astype(jnp.int32)
    pair_live = jnp.any(matches, axis=3)
    touched = jnp.any(member == 1, axis=2)
    enc_view = enc_weight.reshape(N_DP, group_width, NBLK, BLK)
    dec_flat = dec_weight.reshape(NBLK, BLK, features)
    bias_view = enc_bias.reshape(NBLK, BLK)

    def encode(token_rows, chosen_ids, live_mask):
        enc_piece = jnp.take(enc_view, chosen_ids, axis=2).astype(jnp.float32)
        products = jnp.einsum('tid,idrl->irtl', token_rows.reshape(BLK, N_DP, group_width), enc_piece)
        rounded = lax.optimization_barrier(products.astype(jnp.bfloat16)).astype(jnp.float32)
        pre_sum = lax.optimization_barrier(jnp.sum(rounded, axis=0)) + jnp.take(bias_view, chosen_ids, axis=0)[:, None, :]
        activation = (jax.nn.gelu(pre_sum, approximate=True) * live_mask.astype(jnp.float32)[:, None, None]).astype(jnp.bfloat16)
        return (pre_sum, activation)

    def locate(flat_index):
        token_block = flat_index // N_LATENT
        owner_index = flat_index % N_LATENT
        chosen_ids = (owner_index * OWN_BLOCKS + pair_place[token_block, owner_index]).astype(jnp.int32)
        return (token_block, owner_index, chosen_ids)

    def forward_step(rebuilt, flat_index):
        token_block, owner_index, chosen_ids = locate(flat_index)

        def compute(state):
            start = (token_block * BLK).astype(jnp.int32)
            token_rows = lax.dynamic_slice_in_dim(tokens, start, BLK, 0).astype(jnp.float32)
            pre_sum, activation = encode(token_rows, chosen_ids, pair_live[token_block, owner_index])
            dec_piece = jnp.take(dec_flat, chosen_ids, axis=0).astype(jnp.float32)
            partial_value = jnp.einsum('rtl,rld->td', activation.astype(jnp.float32), dec_piece)
            partial_value = lax.optimization_barrier(partial_value.astype(jnp.bfloat16)).astype(jnp.float32)
            current = lax.dynamic_slice_in_dim(state, start, BLK, 0)
            return lax.dynamic_update_slice_in_dim(state, current + partial_value, start, 0)
        return (lax.cond(touched[token_block, owner_index], compute, lambda state: state, rebuilt), None)
    flat_ids = jnp.arange(block_count * N_LATENT, dtype=jnp.int32)
    rebuilt, ignored = lax.scan(forward_step, jnp.zeros((block_count * BLK, features), jnp.float32), flat_ids)
    rebuilt = rebuilt + dec_bias[None, :]
    errors = ((rebuilt - target.astype(jnp.float32)) * 0.03125).astype(jnp.bfloat16)

    def backward_step(accums, flat_index):
        token_block, owner_index, chosen_ids = locate(flat_index)

        def compute(state):
            enc_acc, dec_acc = state
            start = (token_block * BLK).astype(jnp.int32)
            token_rows = lax.dynamic_slice_in_dim(tokens, start, BLK, 0).astype(jnp.float32)
            error_rows = lax.dynamic_slice_in_dim(errors, start, BLK, 0).astype(jnp.float32)
            live_mask = pair_live[token_block, owner_index]
            pre_sum, activation = encode(token_rows, chosen_ids, live_mask)
            dec_piece = jnp.take(dec_flat, chosen_ids, axis=0).astype(jnp.float32)
            products = jnp.einsum('tid,rlid->irtl', error_rows.reshape(BLK, N_DP, group_width), dec_piece.reshape(MB, BLK, N_DP, group_width))
            back_sum = lax.optimization_barrier(jnp.sum(lax.optimization_barrier(products.astype(jnp.bfloat16)).astype(jnp.float32), axis=0))
            grad_pre = (gelu_back(pre_sum, back_sum) * live_mask.astype(jnp.float32)[:, None, None]).astype(jnp.bfloat16).astype(jnp.float32)
            dec_acc = dec_acc.at[chosen_ids].add(jnp.einsum('rtl,td->rld', activation.astype(jnp.float32), error_rows))
            enc_acc = enc_acc.at[chosen_ids].add(jnp.einsum('td,rtl->rdl', token_rows, grad_pre))
            return (enc_acc, dec_acc)
        return (lax.cond(touched[token_block, owner_index], compute, lambda state: state, accums), None)
    start_state = (jnp.zeros((NBLK, features, BLK), jnp.float32), jnp.zeros((NBLK, BLK, features), jnp.float32))
    (enc_acc, dec_acc), ignored = lax.scan(backward_step, start_state, flat_ids)
    grad_enc = jnp.transpose(enc_acc, (1, 0, 2)).reshape(features, NBLK * BLK).astype(jnp.bfloat16)
    grad_dec = dec_acc.reshape(NBLK * BLK, features).astype(jnp.bfloat16)
    return (grad_enc, grad_dec)
```

```python
import functools

import jax
import jax.numpy as jnp
from jax import lax
from jax.experimental import pallas as pl
from jax.experimental.pallas import tpu as pltpu
from jax.sharding import PartitionSpec as P

BLK = 128
MB = 2
ERROR_SCALE = 0.03125
GELU_C = 0.7978845608028654
GELU_A = 0.044715
CODE, TOK, PART, ERR = range(4)
RS_PRE, AG_ACT, RS_BACK, AG_GRAD = range(4)
F32 = jnp.float32
BF16 = jnp.bfloat16


def each(count, body):
    if count <= 4:
        for i in range(count):
            body(i)
    else:
        lax.fori_loop(0, count, lambda i, _: (body(i), None)[1], None)


def rows_at(block):
    return pl.ds(pl.multiple_of(block * BLK, BLK), BLK)


def unpack_source(code):
    bits = code & 255
    total = code >> 8
    two = (bits & (bits - 1)) != 0
    return bits, jnp.where(two, total >> 1, total)


def pair_masks(code, own_blocks):
    bits = code & 255
    rest = bits & (bits - 1)
    first = bits - rest
    return [
        [jnp.where(one == (1 << b), 1.0, 0.0).astype(F32) for b in range(own_blocks)]
        for one in (first, rest)
    ]


def pick(n, codes, tokens, target, outgoing, goal, sem):
    def go(k):
        _, c = unpack_source(codes[k, 0, 0])
        start = pl.ds(pl.multiple_of(c * BLK, BLK), BLK)
        pltpu.make_async_copy(tokens.at[start], outgoing.at[k], sem.at[0, k]).start()
        pltpu.make_async_copy(target.at[start], goal.at[k], sem.at[1, k]).start()

    def done(k):
        pltpu.make_async_copy(outgoing.at[k], outgoing.at[k], sem.at[0, k]).wait()
        pltpu.make_async_copy(goal.at[k], goal.at[k], sem.at[1, k]).wait()

    each(n, go)
    each(n, done)


def kernel(
    n, n_dp, groups,
    codes_hold, outgoing, goal_any, enc_any, dec_any, ebias, dbias,
    genc_any, gdec_any,
    goal, enc, dec, codes_in,
    tok, part_send, part, err_send, err,
    pre_part, pre_in, act, slope, back_part, back_in, grad, act_placed, grad_placed, genc, gdec,
    in_sem, out_sem, z_send, z_recv, d_send, d_recv,
):
    me = lax.axis_index("latent")
    q = lax.axis_index("dp")
    per = n // groups
    rows = BLK // n_dp
    features = enc.shape[0]
    own_blocks = dec.shape[0] // BLK

    loads = [
        pltpu.make_async_copy(src, dst, in_sem.at[i])
        for i, (src, dst) in enumerate(
            ((outgoing.at[me], tok.at[0]), (enc_any, enc), (dec_any, dec), (goal_any, goal))
        )
    ]
    for load in loads:
        load.start()

    barrier = pltpu.get_barrier_semaphore()

    def greet_z(j):
        pl.semaphore_signal(barrier, inc=1, device_id={"latent": lax.rem(me + j + 1, n)})

    def greet_d(j):
        pl.semaphore_signal(barrier, inc=1, device_id={"dp": lax.rem(q + j + 1, n_dp)})

    each(n - 1, greet_z)
    each(n_dp - 1, greet_d)

    def z_copy(phase, src, dst, j):
        return pltpu.make_async_remote_copy(
            src_ref=src,
            dst_ref=dst,
            send_sem=z_send.at[phase, j],
            recv_sem=z_recv.at[phase, n - j],
            device_id={"latent": lax.rem(me + j, n)},
        )

    def z_wait(phase, ref, i):
        pltpu.make_async_remote_copy(
            src_ref=ref,
            dst_ref=ref,
            send_sem=z_send.at[phase, i],
            recv_sem=z_recv.at[phase, i],
            device_id={"latent": lax.rem(me + i, n)},
        ).wait_recv()

    def d_copy(phase, g, src, dst, j):
        return pltpu.make_async_remote_copy(
            src_ref=src,
            dst_ref=dst,
            send_sem=d_send.at[phase, g, j],
            recv_sem=d_recv.at[phase, g, n_dp - j],
            device_id={"dp": lax.rem(q + j, n_dp)},
        )

    def d_wait(phase, g, ref, j):
        pltpu.make_async_remote_copy(
            src_ref=ref,
            dst_ref=ref,
            send_sem=d_send.at[phase, g, j],
            recv_sem=d_recv.at[phase, g, j],
            device_id={"dp": lax.rem(q + j, n_dp)},
        ).wait_recv()

    def span(g):
        return pl.ds(g * per, per)

    def my_rows(p):
        return pl.ds(pl.multiple_of(p * rows, rows), rows)

    def scatter(phase, g, src, dst):
        def go(k):
            j = k + 1
            peer = lax.rem(q + j, n_dp)
            d_copy(phase, g, src.at[span(g), my_rows(peer)], dst.at[n_dp - j, span(g)], j).start()

        each(n_dp - 1, go)

    def scatter_wait(phase, g, dst):
        each(n_dp - 1, lambda k: d_wait(phase, g, dst.at[k + 1, span(g)], k + 1))

    def gather(phase, g, buf):
        mine = buf.at[span(g), my_rows(q)]
        each(n_dp - 1, lambda k: d_copy(phase, g, mine, mine, k + 1).start())

    def gather_wait(phase, g, buf):
        def go(k):
            peer = lax.rem(q + k + 1, n_dp)
            d_wait(phase, g, buf.at[span(g), my_rows(peer)], k + 1)

        each(n_dp - 1, go)

    codes_in[0] = codes_hold[me]
    pl.semaphore_wait(barrier, n - 1 + n_dp - 1)

    def send_tokens(k):
        j = k + 1
        z_copy(CODE, codes_hold.at[lax.rem(me + j, n)], codes_in.at[n - j], j).start()
        z_copy(TOK, outgoing.at[lax.rem(me + j, n)], tok.at[n - j], j).start()

    each(n - 1, send_tokens)

    loads[0].wait()
    loads[1].wait()

    def arrive(g):
        def go(k):
            i = g * per + k

            def get():
                z_wait(CODE, codes_in.at[i], i)
                z_wait(TOK, tok.at[i], i)

            if isinstance(i, int):
                if i > 0:
                    get()
            else:
                pl.when(i > 0)(get)

        each(per, go)

    def at_block(i):
        return pl.ds(i * BLK, BLK) if isinstance(i, int) else rows_at(i)

    def masks_of(i):
        return pair_masks(codes_in[i, 0:1, :], own_blocks)

    def choose(i, full, dst):
        for r, mask in enumerate(masks_of(i)):
            value = mask[0] * full[:, :BLK]
            for b in range(1, own_blocks):
                value = value + mask[b] * full[:, b * BLK:(b + 1) * BLK]
            dst[i, :, r * BLK:(r + 1) * BLK] = value.astype(BF16)

    def place(i, src, dst):
        low, high = masks_of(i)
        first = src[i, :, :BLK].astype(F32)
        second = src[i, :, BLK:].astype(F32)
        for b in range(own_blocks):
            dst[at_block(i), b * BLK:(b + 1) * BLK] = (
                low[b] * first + high[b] * second
            ).astype(BF16)

    def encode(g):
        def go(k):
            i = g * per + k
            choose(i, jnp.dot(tok[i], enc[...], preferred_element_type=F32), pre_part)

        each(per, go)
        scatter(RS_PRE, g, pre_part, pre_in)

    def activate(g):
        scatter_wait(RS_PRE, g, pre_in)

        def go(k):
            i = g * per + k
            total = pre_part[i, my_rows(q), :].astype(F32)
            for j in range(1, n_dp):
                total = total + pre_in[j, i].astype(F32)
            for r, mask in enumerate(masks_of(i)):
                live = sum(mask)
                bias = sum(mask[b] * ebias[b:b + 1, :] for b in range(own_blocks))
                v = total[:, r * BLK:(r + 1) * BLK] + bias
                t = jnp.tanh(GELU_C * (v + GELU_A * (v * v * v)))
                a = 0.5 * v * (1.0 + t)
                s = 0.5 * (1.0 + t) + 0.5 * v * (1.0 - t * t) * (
                    GELU_C * (1.0 + 3.0 * GELU_A * (v * v))
                )
                act[i, my_rows(q), r * BLK:(r + 1) * BLK] = (a * live).astype(BF16)
                slope[i, :, r * BLK:(r + 1) * BLK] = s * live

        each(per, go)
        gather(AG_ACT, g, act)

    def decode(g):
        gather_wait(AG_ACT, g, act)

        def go(k):
            i = g * per + k
            place(i, act, act_placed)
            value = jnp.dot(act_placed[at_block(i), :], dec[...], preferred_element_type=F32)
            value = value.astype(BF16)

            def keep():
                part[0] = value

            def send():
                part_send[i] = value
                z_copy(PART, part_send.at[i], part.at[n - i], i).start()

            if isinstance(i, int):
                keep() if i == 0 else send()
            else:
                pl.when(i == 0)(keep)
                pl.when(i > 0)(send)

        each(per, go)

    encode(0)
    activate(0)
    loads[2].wait()
    decode(0)
    for step in range(1, groups + 2):
        if step < groups:
            arrive(step)
            encode(step)
        if 1 <= step - 1 < groups:
            activate(step - 1)
        if 1 <= step - 2 < groups:
            decode(step - 2)

    loads[3].wait()
    each(n - 1, lambda k: z_wait(PART, part.at[k + 1], k + 1))

    def rebuild(j):
        dest = lax.rem(me + j, n)
        _, c = unpack_source(codes_hold[dest, 0:1, :])

        def weight(o):
            other_bits, other = unpack_source(codes_hold[lax.rem(me + o, n), 0:1, :])
            same = jnp.where((other_bits != 0) & (other == c), 1.0, 0.0).astype(F32)
            return jnp.concatenate([same] * (features // BLK), axis=1)

        @pl.loop(0, BLK // 32)
        def _(r):
            at = pl.ds(pl.multiple_of(r * 32, 32), 32)

            def add(o, total):
                return total + weight(o) * part[o, at, :].astype(F32)

            total = jnp.zeros((32, features), F32)
            if n <= 4:
                for o in range(n):
                    total = add(o, total)
            else:
                total = lax.fori_loop(0, n, add, total)
            wanted = goal[dest, at, :].astype(F32)
            error = (((total + dbias[...]) - wanted) * ERROR_SCALE).astype(BF16)
            if isinstance(j, int) and j == 0:
                err[0, at, :] = error
            else:
                err_send[j, at, :] = error

    def rebuild_send(k):
        rebuild(k + 1)
        z_copy(ERR, err_send.at[k + 1], err.at[n - (k + 1)], k + 1).start()

    each(n - 1, rebuild_send)
    rebuild(0)

    def push_back(g):
        def go(k):
            i = g * per + k

            def get():
                z_wait(ERR, err.at[i], i)

            if isinstance(i, int):
                if i > 0:
                    get()
            else:
                pl.when(i > 0)(get)
            full = lax.dot_general(
                err[i], dec[...], (((1,), (1,)), ((), ())), preferred_element_type=F32
            )
            choose(i, full, back_part)

        each(per, go)
        scatter(RS_BACK, g, back_part, back_in)

    def make_grad(g):
        scatter_wait(RS_BACK, g, back_in)

        def go(k):
            i = g * per + k
            total = back_part[i, my_rows(q), :].astype(F32)
            for j in range(1, n_dp):
                total = total + back_in[j, i].astype(F32)
            grad[i, my_rows(q), :] = (total * slope[i]).astype(BF16)

        each(per, go)
        gather(AG_GRAD, g, grad)

    for step in range(groups):
        push_back(step)
        if step >= 1:
            make_grad(step - 1)
    make_grad(groups - 1)

    every = err[...].reshape(n * BLK, features)
    for b in range(own_blocks):
        value = lax.dot_general(
            act_placed[:, b * BLK:(b + 1) * BLK], every,
            (((0,), (0,)), ((), ())), preferred_element_type=F32,
        )
        gdec[b * BLK:(b + 1) * BLK, :] = value.astype(BF16)
    store_dec = pltpu.make_async_copy(gdec, gdec_any, out_sem.at[0])
    store_dec.start()

    for g in range(groups):
        gather_wait(AG_GRAD, g, grad)
        each(per, lambda k, g=g: place(g * per + k, grad, grad_placed))
    every = tok[...].reshape(n * BLK, features)
    for f in range(0, features, BLK):
        value = lax.dot_general(
            every[:, f:f + BLK], grad_placed[...],
            (((0,), (0,)), ((), ())), preferred_element_type=F32,
        )
        genc[f:f + BLK, :] = value.astype(BF16)
    store_enc = pltpu.make_async_copy(genc, genc_any, out_sem.at[1])
    store_enc.start()

    def settle(k):
        j = k + 1
        z_copy(CODE, codes_hold.at[lax.rem(me + j, n)], codes_in.at[n - j], j).wait_send()
        z_copy(TOK, outgoing.at[lax.rem(me + j, n)], tok.at[n - j], j).wait_send()
        z_copy(PART, part_send.at[j], part.at[n - j], j).wait_send()
        z_copy(ERR, err_send.at[j], err.at[n - j], j).wait_send()

    each(n - 1, settle)

    for g in range(groups):
        def settle_d(k, g=g):
            j = k + 1
            peer = lax.rem(q + j, n_dp)
            for phase, src, dst in ((RS_PRE, pre_part, pre_in), (RS_BACK, back_part, back_in)):
                d_copy(
                    phase, g, src.at[span(g), my_rows(peer)], dst.at[n_dp - j, span(g)], j
                ).wait_send()
            for phase, buf in ((AG_ACT, act), (AG_GRAD, grad)):
                mine = buf.at[span(g), my_rows(q)]
                d_copy(phase, g, mine, mine, j).wait_send()

        each(n_dp - 1, settle_d)
    store_dec.wait()
    store_enc.wait()


def local(tokens, target, enc_weight, dec_weight, enc_bias, dec_bias, active, counts):
    n = lax.axis_size("latent")
    n_dp = lax.axis_size("dp")
    groups = min(n, 4)
    features = tokens.shape[1]
    own = enc_weight.shape[1]
    own_blocks = own // BLK
    rows = BLK // n_dp
    position = lax.broadcasted_iota(jnp.int32, active.shape, 1)
    live = position < counts[:, None]
    value = (1 << (active % own_blocks)) + 256 * lax.broadcasted_iota(jnp.int32, active.shape, 0)
    owner_ids = jnp.arange(n, dtype=jnp.int32)
    mask = live[None] & ((active // own_blocks)[None] == owner_ids[:, None, None])
    codes = jnp.sum(jnp.where(mask, value[None], 0), axis=(1, 2))
    codes = jnp.broadcast_to(codes[:, None, None], (n, 8, BLK)).astype(jnp.int32)
    vmem = pl.BlockSpec(memory_space=pltpu.VMEM)
    hbm = pl.BlockSpec(memory_space=pl.ANY)
    slots = (n, BLK, features)
    pairs = (n, BLK, MB * BLK)
    pieces = (n_dp, n, rows, MB * BLK)
    dma = pltpu.SemaphoreType.DMA
    chosen = jax.ShapeDtypeStruct(slots, BF16)
    outgoing, goal = pl.pallas_call(
        functools.partial(pick, n),
        out_shape=(chosen, chosen),
        in_specs=[pl.BlockSpec(memory_space=pltpu.SMEM), hbm, hbm],
        out_specs=(hbm, hbm),
        scratch_shapes=[dma((2, n))],
    )(codes, tokens, target)
    return pl.pallas_call(
        functools.partial(kernel, n, n_dp, groups),
        out_shape=(
            jax.ShapeDtypeStruct(enc_weight.shape, BF16),
            jax.ShapeDtypeStruct(dec_weight.shape, BF16),
        ),
        in_specs=[vmem, hbm, hbm, hbm, hbm, vmem, vmem],
        out_specs=(hbm, hbm),
        scratch_shapes=[
            pltpu.VMEM(slots, BF16),
            pltpu.VMEM(enc_weight.shape, BF16),
            pltpu.VMEM(dec_weight.shape, BF16),
            pltpu.VMEM((n, 8, BLK), jnp.int32),
            pltpu.VMEM(slots, BF16),
            pltpu.VMEM(slots, BF16),
            pltpu.VMEM(slots, BF16),
            pltpu.VMEM(slots, BF16),
            pltpu.VMEM(slots, BF16),
            pltpu.VMEM(pairs, BF16),
            pltpu.VMEM(pieces, BF16),
            pltpu.VMEM(pairs, BF16),
            pltpu.VMEM((n, rows, MB * BLK), F32),
            pltpu.VMEM(pairs, BF16),
            pltpu.VMEM(pieces, BF16),
            pltpu.VMEM(pairs, BF16),
            pltpu.VMEM((n * BLK, own), BF16),
            pltpu.VMEM((n * BLK, own), BF16),
            pltpu.VMEM(enc_weight.shape, BF16),
            pltpu.VMEM(dec_weight.shape, BF16),
            dma((4,)),
            dma((2,)),
            dma((4, n)),
            dma((4, n)),
            dma((4, groups, n_dp)),
            dma((4, groups, n_dp)),
        ],
        compiler_params=pltpu.CompilerParams(
            collective_id=0, has_side_effects=True, vmem_limit_bytes=56 * 1024 * 1024
        ),
    )(
        codes, outgoing, goal, enc_weight, dec_weight,
        enc_bias.reshape(own_blocks, BLK), dec_bias.reshape(1, features),
    )


def solution(mesh):
    placed = (
        P(("parts", "latent"), "dp"),
        P(("parts", "latent"), "dp"),
        P(("parts", "dp"), "latent"),
        P(("parts", "latent"), "dp"),
        P(("parts", "latent")),
        P(("parts", "dp")),
        P(("parts", "latent"), None),
        P(("parts", "latent")),
    )
    return jax.shard_map(
        local,
        mesh=mesh,
        in_specs=placed,
        out_specs=(P(("parts", "dp"), "latent"), P(("parts", "latent"), "dp")),
        check_vma=False,
    )
```

```python
import functools

import jax
import jax.numpy as jnp
from jax import lax
from jax.experimental import pallas as pl
from jax.experimental.pallas import tpu as pltpu
from jax.sharding import PartitionSpec as P

BLK = 128
MB = 2
ERROR_SCALE = 0.03125
GELU_C = 0.7978845608028654
GELU_A = 0.044715
TOK, PART, ERR = range(3)
RS_PRE, AG_ACT, RS_BACK, AG_GRAD = range(4)
F32 = jnp.float32
BF16 = jnp.bfloat16


def each(count, body):
    if count <= 4:
        for i in range(count):
            body(i)
    else:
        lax.fori_loop(0, count, lambda i, _: (body(i), None)[1], None)


def pair_masks(code, own_blocks):
    bits = code & 255
    rest = bits & (bits - 1)
    first = bits - rest
    return [
        [jnp.where(one == (1 << b), 1.0, 0.0).astype(F32) for b in range(own_blocks)]
        for one in (first, rest)
    ]


def kernel(
    n, n_dp, halves,
    counts, active, tokens_any, target_any, enc_any, dec_any, ebias, dbias,
    genc_any, gdec_any,
    tokens, target, enc, dec, codes_out, codes_in,
    tok_send, goal, tok, part_send, part, err_send, err,
    pre_part, pre_in, act, slope, back_part, back_in, grad, act_placed, grad_placed, genc, gdec,
    in_sem, out_sem, c_send, c_recv, z_send, z_recv, d_send, d_recv,
):
    me = lax.axis_index("latent")
    q = lax.axis_index("dp")
    high = BLK // halves
    rows = high // n_dp
    features = enc.shape[0]
    own_blocks = dec.shape[0] // BLK
    blocks, width = active.shape
    tile = min(n, 4)

    loads = [
        pltpu.make_async_copy(src, dst, in_sem.at[i])
        for i, (src, dst) in enumerate(
            ((tokens_any, tokens), (enc_any, enc), (dec_any, dec), (target_any, target))
        )
    ]
    for load in loads:
        load.start()

    barrier = pltpu.get_barrier_semaphore()

    def greet_z(j):
        pl.semaphore_signal(barrier, inc=1, device_id={"latent": lax.rem(me + j + 1, n)})

    def greet_d(j):
        pl.semaphore_signal(barrier, inc=1, device_id={"dp": lax.rem(q + j + 1, n_dp)})

    each(n - 1, greet_z)
    each(n_dp - 1, greet_d)

    row = lax.broadcasted_iota(jnp.int32, (blocks, width), 0)
    column = lax.broadcasted_iota(jnp.int32, (blocks, width), 1)
    used = jnp.zeros((blocks, width), jnp.int32)
    for t in range(blocks):
        used = jnp.where(row == t, counts[t], used)
    ids = active[...]
    place_bit = jnp.zeros((blocks, width), jnp.int32)
    for b in range(own_blocks):
        place_bit = jnp.where(ids % own_blocks == b, 1 << b, place_bit)
    value = (place_bit + 256 * row).astype(F32)
    owner = ids // own_blocks

    def encode_owner(k):
        total = jnp.where((column < used) & (owner == k), value, 0.0)
        total = jnp.sum(jnp.sum(total, axis=1, keepdims=True), axis=0, keepdims=True)
        codes_out[k] = jnp.broadcast_to(total, (8, BLK)).astype(jnp.int32)

    each(n, encode_owner)
    codes_in[0] = codes_out[me]

    def source(j):
        code = codes_out[lax.rem(me + j, n), 0:1, :]
        bits = code & 255
        total = code >> 8
        two = (bits & (bits - 1)) != 0
        return bits, jnp.where(two, total >> 1, total)

    def wide(mask):
        return jnp.concatenate([mask] * (features // BLK), axis=1)

    def chosen_rows(j, ref, at):
        _, c = source(j)
        total = None
        for t in range(blocks):
            weight = wide(jnp.where(c == t, 1.0, 0.0).astype(BF16))
            piece = weight * ref[t * BLK + at:t * BLK + at + 32, :]
            total = piece if total is None else total + piece
        return total

    def z_copy(phase, h, src, dst, j):
        return pltpu.make_async_remote_copy(
            src_ref=src.at[h, j],
            dst_ref=dst.at[h, n - j],
            send_sem=z_send.at[phase, h, j],
            recv_sem=z_recv.at[phase, h, n - j],
            device_id={"latent": lax.rem(me + j, n)},
        )

    def c_copy(j):
        return pltpu.make_async_remote_copy(
            src_ref=codes_out.at[lax.rem(me + j, n)],
            dst_ref=codes_in.at[n - j],
            send_sem=c_send.at[j],
            recv_sem=c_recv.at[n - j],
            device_id={"latent": lax.rem(me + j, n)},
        )

    def z_wait(phase, h, ref):
        each(n - 1, lambda k: pltpu.make_async_remote_copy(
            src_ref=ref.at[h, k + 1],
            dst_ref=ref.at[h, k + 1],
            send_sem=z_send.at[phase, h, k + 1],
            recv_sem=z_recv.at[phase, h, k + 1],
            device_id={"latent": lax.rem(me + k + 1, n)},
        ).wait_recv())

    def c_wait(j):
        pltpu.make_async_remote_copy(
            src_ref=codes_in.at[j],
            dst_ref=codes_in.at[j],
            send_sem=c_send.at[j],
            recv_sem=c_recv.at[j],
            device_id={"latent": lax.rem(me + j, n)},
        ).wait_recv()

    def d_copy(phase, h, src, dst, j):
        return pltpu.make_async_remote_copy(
            src_ref=src,
            dst_ref=dst,
            send_sem=d_send.at[phase, h, j],
            recv_sem=d_recv.at[phase, h, n_dp - j],
            device_id={"dp": lax.rem(q + j, n_dp)},
        )

    def d_wait(phase, h, ref, j):
        pltpu.make_async_remote_copy(
            src_ref=ref,
            dst_ref=ref,
            send_sem=d_send.at[phase, h, j],
            recv_sem=d_recv.at[phase, h, j],
            device_id={"dp": lax.rem(q + j, n_dp)},
        ).wait_recv()

    every = pl.ds(0, n)

    def dp_rows(p):
        return pl.ds(pl.multiple_of(p * rows, rows), rows)

    def scatter_copy(phase, h, src, dst, j):
        peer = lax.rem(q + j, n_dp)
        return d_copy(phase, h, src.at[h, every, dp_rows(peer)], dst.at[h, n_dp - j], j)

    def scatter(phase, h, src, dst):
        each(n_dp - 1, lambda k: scatter_copy(phase, h, src, dst, k + 1).start())

    def scatter_wait(phase, h, dst):
        each(n_dp - 1, lambda k: d_wait(phase, h, dst.at[h, k + 1], k + 1))

    def gather_copy(phase, h, buf, j):
        mine = buf.at[h, every, dp_rows(q)]
        return d_copy(phase, h, mine, mine, j)

    def gather(phase, h, buf):
        each(n_dp - 1, lambda k: gather_copy(phase, h, buf, k + 1).start())

    def gather_wait(phase, h, buf):
        each(n_dp - 1, lambda k: d_wait(
            phase, h, buf.at[h, every, dp_rows(lax.rem(q + k + 1, n_dp))], k + 1
        ))

    loads[0].wait()
    for h in range(halves):
        def stage(j, h=h):
            for at in range(0, high, 32):
                tok_send[h, j, at:at + 32, :] = chosen_rows(j, tokens, h * high + at)

        each(n - 1, lambda k: stage(k + 1))
        if h == 0:
            pl.semaphore_wait(barrier, n - 1 + n_dp - 1)
            each(n - 1, lambda k: c_copy(k + 1).start())
        each(n - 1, lambda k, h=h: z_copy(TOK, h, tok_send, tok, k + 1).start())
    for h in range(halves):
        for at in range(0, high, 32):
            tok[h, 0, at:at + 32, :] = chosen_rows(0, tokens, h * high + at)
    loads[3].wait()

    def aim(j):
        for h in range(halves):
            for at in range(0, high, 32):
                goal[h, j, at:at + 32, :] = chosen_rows(j, target, h * high + at)

    each(n, aim)
    loads[1].wait()
    each(n - 1, lambda k: c_wait(k + 1))
    loads[2].wait()

    def masks_of(i):
        return pair_masks(codes_in[i, 0:1, :], own_blocks)

    def tiles(body):
        each(n // tile, lambda k: body(k * tile))

    def stack(h, buf, first):
        block = buf[h, pl.ds(first, tile)]
        return block.reshape(tile * high, block.shape[-1])

    def choose(h, i, full, dst):
        for r, mask in enumerate(masks_of(i)):
            total = mask[0] * full[:, :BLK]
            for b in range(1, own_blocks):
                total = total + mask[b] * full[:, b * BLK:(b + 1) * BLK]
            dst[h, i, :, r * BLK:(r + 1) * BLK] = total.astype(BF16)

    def place(h, i, src, dst):
        low, rest = masks_of(i)
        first = src[h, i, :, :BLK].astype(F32)
        second = src[h, i, :, BLK:].astype(F32)
        for b in range(own_blocks):
            dst[h, i, :, b * BLK:(b + 1) * BLK] = (
                low[b] * first + rest[b] * second
            ).astype(BF16)

    def encode(h):
        z_wait(TOK, h, tok)

        def go(first):
            full = jnp.dot(stack(h, tok, first), enc[...], preferred_element_type=F32)
            for k in range(tile):
                choose(h, first + k, full[k * high:(k + 1) * high], pre_part)

        tiles(go)
        scatter(RS_PRE, h, pre_part, pre_in)

    def activate(h):
        scatter_wait(RS_PRE, h, pre_in)

        def go(i):
            total = pre_part[h, i, dp_rows(q), :].astype(F32)
            for j in range(1, n_dp):
                total = total + pre_in[h, j, i].astype(F32)
            for r, mask in enumerate(masks_of(i)):
                live = sum(mask)
                bias = sum(mask[b] * ebias[b:b + 1, :] for b in range(own_blocks))
                v = total[:, r * BLK:(r + 1) * BLK] + bias
                t = jnp.tanh(GELU_C * (v + GELU_A * (v * v * v)))
                a = 0.5 * v * (1.0 + t)
                s = 0.5 * (1.0 + t) + 0.5 * v * (1.0 - t * t) * (
                    GELU_C * (1.0 + 3.0 * GELU_A * (v * v))
                )
                act[h, i, dp_rows(q), r * BLK:(r + 1) * BLK] = (a * live).astype(BF16)
                slope[h, i, :, r * BLK:(r + 1) * BLK] = s * live

        each(n, go)
        gather(AG_ACT, h, act)

    def decode(h):
        gather_wait(AG_ACT, h, act)

        def go(first):
            for k in range(tile):
                place(h, first + k, act, act_placed)
            full = jnp.dot(stack(h, act_placed, first), dec[...], preferred_element_type=F32)
            full = full.astype(BF16)
            for k in range(tile):
                part_send[h, first + k] = full[k * high:(k + 1) * high]

        tiles(go)
        part[h, 0] = part_send[h, 0]
        each(n - 1, lambda k: z_copy(PART, h, part_send, part, k + 1).start())

    for h in range(halves):
        encode(h)
        activate(h)
        decode(h)

    def rebuild(h):
        z_wait(PART, h, part)

        def go(j):
            _, c = source(j)

            def weight(o):
                other_bits, other = source(o)
                return wide(jnp.where((other_bits != 0) & (other == c), 1.0, 0.0).astype(F32))

            for at in range(0, high, 16):
                def add(o, total, at=at):
                    return total + weight(o) * part[h, o, at:at + 16, :].astype(F32)

                total = jnp.zeros((16, features), F32)
                if n <= 4:
                    for o in range(n):
                        total = add(o, total)
                else:
                    total = lax.fori_loop(0, n, add, total)
                wanted = goal[h, j, at:at + 16, :].astype(F32)
                err_send[h, j, at:at + 16, :] = (
                    ((total + dbias[...]) - wanted) * ERROR_SCALE
                ).astype(BF16)

        def send(k):
            go(k + 1)
            z_copy(ERR, h, err_send, err, k + 1).start()

        each(n - 1, send)
        go(0)
        err[h, 0] = err_send[h, 0]

    for h in range(halves):
        rebuild(h)

    def push_back(h):
        z_wait(ERR, h, err)

        def go(first):
            full = lax.dot_general(
                stack(h, err, first), dec[...], (((1,), (1,)), ((), ())),
                preferred_element_type=F32,
            )
            for k in range(tile):
                choose(h, first + k, full[k * high:(k + 1) * high], back_part)

        tiles(go)
        scatter(RS_BACK, h, back_part, back_in)

    def make_grad(h):
        scatter_wait(RS_BACK, h, back_in)

        def go(i):
            total = back_part[h, i, dp_rows(q), :].astype(F32)
            for j in range(1, n_dp):
                total = total + back_in[h, j, i].astype(F32)
            grad[h, i, dp_rows(q), :] = (total * slope[h, i]).astype(BF16)

        each(n, go)
        gather(AG_GRAD, h, grad)

    for h in range(halves):
        push_back(h)
        make_grad(h)

    depth = halves * n * high
    errors = err[...].reshape(depth, features)
    for b in range(own_blocks):
        left = act_placed[:, :, :, b * BLK:(b + 1) * BLK].reshape(depth, BLK)
        gdec[b * BLK:(b + 1) * BLK, :] = lax.dot_general(
            left, errors, (((0,), (0,)), ((), ())), preferred_element_type=F32
        ).astype(BF16)
    store_dec = pltpu.make_async_copy(gdec, gdec_any, out_sem.at[0])
    store_dec.start()

    for h in range(halves):
        gather_wait(AG_GRAD, h, grad)
        each(n, lambda i, h=h: place(h, i, grad, grad_placed))
    right = grad_placed[...].reshape(depth, own_blocks * BLK)
    for f in range(0, features, BLK):
        left = tok[:, :, :, f:f + BLK].reshape(depth, BLK)
        genc[f:f + BLK, :] = lax.dot_general(
            left, right, (((0,), (0,)), ((), ())), preferred_element_type=F32
        ).astype(BF16)
    store_enc = pltpu.make_async_copy(genc, genc_any, out_sem.at[1])
    store_enc.start()

    each(n - 1, lambda k: c_copy(k + 1).wait_send())
    for h in range(halves):
        def settle_z(k, h=h):
            for phase, src, dst in (
                (TOK, tok_send, tok), (PART, part_send, part), (ERR, err_send, err)
            ):
                z_copy(phase, h, src, dst, k + 1).wait_send()

        def settle_d(k, h=h):
            for phase, src, dst in ((RS_PRE, pre_part, pre_in), (RS_BACK, back_part, back_in)):
                scatter_copy(phase, h, src, dst, k + 1).wait_send()
            for phase, buf in ((AG_ACT, act), (AG_GRAD, grad)):
                gather_copy(phase, h, buf, k + 1).wait_send()

        each(n - 1, settle_z)
        each(n_dp - 1, settle_d)
    store_dec.wait()
    store_enc.wait()


def local(tokens, target, enc_weight, dec_weight, enc_bias, dec_bias, active, counts):
    n = lax.axis_size("latent")
    n_dp = lax.axis_size("dp")
    halves = max(1, BLK // (16 * n_dp))
    features = tokens.shape[1]
    own = enc_weight.shape[1]
    high = BLK // halves
    rows = high // n_dp
    vmem = pl.BlockSpec(memory_space=pltpu.VMEM)
    smem = pl.BlockSpec(memory_space=pltpu.SMEM)
    hbm = pl.BlockSpec(memory_space=pl.ANY)
    slots = pltpu.VMEM((halves, n, high, features), BF16)
    pairs = pltpu.VMEM((halves, n, high, MB * BLK), BF16)
    pieces = pltpu.VMEM((halves, n_dp, n, rows, MB * BLK), BF16)
    placed = pltpu.VMEM((halves, n, high, own), BF16)
    codes = pltpu.VMEM((n, 8, BLK), jnp.int32)
    dma = pltpu.SemaphoreType.DMA
    return pl.pallas_call(
        functools.partial(kernel, n, n_dp, halves),
        out_shape=(
            jax.ShapeDtypeStruct(enc_weight.shape, BF16),
            jax.ShapeDtypeStruct(dec_weight.shape, BF16),
        ),
        in_specs=[smem, vmem, hbm, hbm, hbm, hbm, vmem, vmem],
        out_specs=(hbm, hbm),
        scratch_shapes=[
            pltpu.VMEM(tokens.shape, BF16),
            pltpu.VMEM(target.shape, BF16),
            pltpu.VMEM(enc_weight.shape, BF16),
            pltpu.VMEM(dec_weight.shape, BF16),
            codes,
            codes,
            slots,
            slots,
            slots,
            slots,
            slots,
            slots,
            slots,
            pairs,
            pieces,
            pairs,
            pltpu.VMEM((halves, n, rows, MB * BLK), F32),
            pairs,
            pieces,
            pairs,
            placed,
            placed,
            pltpu.VMEM(enc_weight.shape, BF16),
            pltpu.VMEM(dec_weight.shape, BF16),
            dma((4,)),
            dma((2,)),
            dma((n,)),
            dma((n,)),
            dma((3, halves, n)),
            dma((3, halves, n)),
            dma((4, halves, n_dp)),
            dma((4, halves, n_dp)),
        ],
        compiler_params=pltpu.CompilerParams(
            collective_id=0, has_side_effects=True, vmem_limit_bytes=60 * 1024 * 1024
        ),
    )(
        counts, active, tokens, target, enc_weight, dec_weight,
        enc_bias.reshape(own // BLK, BLK), dec_bias.reshape(1, features),
    )


def solution(mesh):
    placed = (
        P(("parts", "latent"), "dp"),
        P(("parts", "latent"), "dp"),
        P(("parts", "dp"), "latent"),
        P(("parts", "latent"), "dp"),
        P(("parts", "latent")),
        P(("parts", "dp")),
        P(("parts", "latent"), None),
        P(("parts", "latent")),
    )
    return jax.shard_map(
        local,
        mesh=mesh,
        in_specs=placed,
        out_specs=(P(("parts", "dp"), "latent"), P(("parts", "latent"), "dp")),
        check_vma=False,
    )
```

```python
import functools

import jax
import jax.numpy as jnp
from jax import lax
from jax.experimental import pallas as pl
from jax.experimental.pallas import tpu as pltpu
from jax.sharding import PartitionSpec as P

BLK = 128
MB = 2
ERROR_SCALE = 0.03125
GELU_C = 0.7978845608028654
GELU_A = 0.044715
TOK, PART, ERR = range(3)
RS_PRE, AG_ACT, RS_BACK, AG_GRAD = range(4)
F32 = jnp.float32
BF16 = jnp.bfloat16


def each(count, body):
    if count <= 4:
        for i in range(count):
            body(i)
    else:
        lax.fori_loop(0, count, lambda i, _: (body(i), None)[1], None)


def pair_masks(code, own_blocks):
    bits = code & 255
    rest = bits & (bits - 1)
    first = bits - rest
    return [
        [jnp.where(one == (1 << b), 1.0, 0.0).astype(F32) for b in range(own_blocks)]
        for one in (first, rest)
    ]


def kernel(
    n, n_dp, halves,
    counts, active, tokens_any, target_any, enc_any, dec_any, ebias, dbias,
    tok_any, err_any, act_any, grad_any,
    tokens, target, enc, dec, codes_out, codes_in,
    tok_send, goal, tok, part_send, part, err_send, err,
    pre_part, pre_in, act, slope, back_part, back_in, grad, act_placed, grad_placed,
    in_sem, out_sem, c_send, c_recv, z_send, z_recv, d_send, d_recv,
):
    me = lax.axis_index("latent")
    q = lax.axis_index("dp")
    high = BLK // halves
    rows = high // n_dp
    features = enc.shape[0]
    own_blocks = dec.shape[0] // BLK
    blocks, width = active.shape
    tile = min(n, 4)

    loads = [
        pltpu.make_async_copy(src, dst, in_sem.at[i])
        for i, (src, dst) in enumerate(
            ((tokens_any, tokens), (enc_any, enc), (dec_any, dec), (target_any, target))
        )
    ]
    for load in loads:
        load.start()

    barrier = pltpu.get_barrier_semaphore()

    def greet_z(j):
        pl.semaphore_signal(barrier, inc=1, device_id={"latent": lax.rem(me + j + 1, n)})

    def greet_d(j):
        pl.semaphore_signal(barrier, inc=1, device_id={"dp": lax.rem(q + j + 1, n_dp)})

    each(n - 1, greet_z)
    each(n_dp - 1, greet_d)

    row = lax.broadcasted_iota(jnp.int32, (blocks, width), 0)
    column = lax.broadcasted_iota(jnp.int32, (blocks, width), 1)
    used = jnp.zeros((blocks, width), jnp.int32)
    for t in range(blocks):
        used = jnp.where(row == t, counts[t], used)
    ids = active[...]
    place_bit = jnp.zeros((blocks, width), jnp.int32)
    for b in range(own_blocks):
        place_bit = jnp.where(ids % own_blocks == b, 1 << b, place_bit)
    value = (place_bit + 256 * row).astype(F32)
    owner = ids // own_blocks

    def encode_owner(k):
        total = jnp.where((column < used) & (owner == k), value, 0.0)
        total = jnp.sum(jnp.sum(total, axis=1, keepdims=True), axis=0, keepdims=True)
        codes_out[k] = jnp.broadcast_to(total, (8, BLK)).astype(jnp.int32)

    each(n, encode_owner)
    codes_in[0] = codes_out[me]

    def source(j):
        code = codes_out[lax.rem(me + j, n), 0:1, :]
        bits = code & 255
        total = code >> 8
        two = (bits & (bits - 1)) != 0
        return bits, jnp.where(two, total >> 1, total)

    def wide(mask):
        return jnp.concatenate([mask] * (features // BLK), axis=1)

    def chosen_rows(j, ref, at):
        _, c = source(j)
        total = None
        for t in range(blocks):
            weight = wide(jnp.where(c == t, 1.0, 0.0).astype(BF16))
            piece = weight * ref[t * BLK + at:t * BLK + at + 32, :]
            total = piece if total is None else total + piece
        return total

    def z_copy(phase, h, src, dst, j):
        return pltpu.make_async_remote_copy(
            src_ref=src.at[h, j],
            dst_ref=dst.at[h, n - j],
            send_sem=z_send.at[phase, h, j],
            recv_sem=z_recv.at[phase, h, n - j],
            device_id={"latent": lax.rem(me + j, n)},
        )

    def c_copy(j):
        return pltpu.make_async_remote_copy(
            src_ref=codes_out.at[lax.rem(me + j, n)],
            dst_ref=codes_in.at[n - j],
            send_sem=c_send.at[j],
            recv_sem=c_recv.at[n - j],
            device_id={"latent": lax.rem(me + j, n)},
        )

    def z_wait(phase, h, ref):
        each(n - 1, lambda k: pltpu.make_async_remote_copy(
            src_ref=ref.at[h, k + 1],
            dst_ref=ref.at[h, k + 1],
            send_sem=z_send.at[phase, h, k + 1],
            recv_sem=z_recv.at[phase, h, k + 1],
            device_id={"latent": lax.rem(me + k + 1, n)},
        ).wait_recv())

    def c_wait(j):
        pltpu.make_async_remote_copy(
            src_ref=codes_in.at[j],
            dst_ref=codes_in.at[j],
            send_sem=c_send.at[j],
            recv_sem=c_recv.at[j],
            device_id={"latent": lax.rem(me + j, n)},
        ).wait_recv()

    def d_copy(phase, h, src, dst, j):
        return pltpu.make_async_remote_copy(
            src_ref=src,
            dst_ref=dst,
            send_sem=d_send.at[phase, h, j],
            recv_sem=d_recv.at[phase, h, n_dp - j],
            device_id={"dp": lax.rem(q + j, n_dp)},
        )

    def d_wait(phase, h, ref, j):
        pltpu.make_async_remote_copy(
            src_ref=ref,
            dst_ref=ref,
            send_sem=d_send.at[phase, h, j],
            recv_sem=d_recv.at[phase, h, j],
            device_id={"dp": lax.rem(q + j, n_dp)},
        ).wait_recv()

    every = pl.ds(0, n)

    def dp_rows(p):
        return pl.ds(pl.multiple_of(p * rows, rows), rows)

    def scatter_copy(phase, h, src, dst, j):
        peer = lax.rem(q + j, n_dp)
        return d_copy(phase, h, src.at[h, every, dp_rows(peer)], dst.at[h, n_dp - j], j)

    def scatter(phase, h, src, dst):
        each(n_dp - 1, lambda k: scatter_copy(phase, h, src, dst, k + 1).start())

    def scatter_wait(phase, h, dst):
        each(n_dp - 1, lambda k: d_wait(phase, h, dst.at[h, k + 1], k + 1))

    def gather_copy(phase, h, buf, j):
        mine = buf.at[h, every, dp_rows(q)]
        return d_copy(phase, h, mine, mine, j)

    def gather(phase, h, buf):
        each(n_dp - 1, lambda k: gather_copy(phase, h, buf, k + 1).start())

    def gather_wait(phase, h, buf):
        each(n_dp - 1, lambda k: d_wait(
            phase, h, buf.at[h, every, dp_rows(lax.rem(q + k + 1, n_dp))], k + 1
        ))

    loads[0].wait()
    for h in range(halves):
        def stage(j, h=h):
            for at in range(0, high, 32):
                tok_send[h, j, at:at + 32, :] = chosen_rows(j, tokens, h * high + at)

        each(n - 1, lambda k: stage(k + 1))
        if h == 0:
            pl.semaphore_wait(barrier, n - 1 + n_dp - 1)
            each(n - 1, lambda k: c_copy(k + 1).start())
        each(n - 1, lambda k, h=h: z_copy(TOK, h, tok_send, tok, k + 1).start())
    for h in range(halves):
        for at in range(0, high, 32):
            tok[h, 0, at:at + 32, :] = chosen_rows(0, tokens, h * high + at)
    loads[3].wait()

    def aim(j):
        for h in range(halves):
            for at in range(0, high, 32):
                goal[h, j, at:at + 32, :] = chosen_rows(j, target, h * high + at)

    each(n, aim)
    loads[1].wait()
    each(n - 1, lambda k: c_wait(k + 1))
    loads[2].wait()

    def store(which, h, src, dst):
        return pltpu.make_async_copy(src.at[h], dst.at[h], out_sem.at[which, h])

    def masks_of(i):
        return pair_masks(codes_in[i, 0:1, :], own_blocks)

    def tiles(body):
        each(n // tile, lambda k: body(k * tile))

    def stack(h, buf, first):
        block = buf[h, pl.ds(first, tile)]
        return block.reshape(tile * high, block.shape[-1])

    def choose(h, i, full, dst):
        for r, mask in enumerate(masks_of(i)):
            total = mask[0] * full[:, :BLK]
            for b in range(1, own_blocks):
                total = total + mask[b] * full[:, b * BLK:(b + 1) * BLK]
            dst[h, i, :, r * BLK:(r + 1) * BLK] = total.astype(BF16)

    def place(h, i, src, dst):
        low, rest = masks_of(i)
        first = src[h, i, :, :BLK].astype(F32)
        second = src[h, i, :, BLK:].astype(F32)
        for b in range(own_blocks):
            dst[h, i, :, b * BLK:(b + 1) * BLK] = (
                low[b] * first + rest[b] * second
            ).astype(BF16)

    def encode(h):
        z_wait(TOK, h, tok)

        def go(first):
            full = jnp.dot(stack(h, tok, first), enc[...], preferred_element_type=F32)
            for k in range(tile):
                choose(h, first + k, full[k * high:(k + 1) * high], pre_part)

        tiles(go)
        scatter(RS_PRE, h, pre_part, pre_in)

    def activate(h):
        scatter_wait(RS_PRE, h, pre_in)

        def go(i):
            total = pre_part[h, i, dp_rows(q), :].astype(F32)
            for j in range(1, n_dp):
                total = total + pre_in[h, j, i].astype(F32)
            for r, mask in enumerate(masks_of(i)):
                live = sum(mask)
                bias = sum(mask[b] * ebias[b:b + 1, :] for b in range(own_blocks))
                v = total[:, r * BLK:(r + 1) * BLK] + bias
                t = jnp.tanh(GELU_C * (v + GELU_A * (v * v * v)))
                a = 0.5 * v * (1.0 + t)
                s = 0.5 * (1.0 + t) + 0.5 * v * (1.0 - t * t) * (
                    GELU_C * (1.0 + 3.0 * GELU_A * (v * v))
                )
                act[h, i, dp_rows(q), r * BLK:(r + 1) * BLK] = (a * live).astype(BF16)
                slope[h, i, :, r * BLK:(r + 1) * BLK] = s * live

        each(n, go)
        gather(AG_ACT, h, act)

    def decode(h):
        gather_wait(AG_ACT, h, act)

        def go(first):
            for k in range(tile):
                place(h, first + k, act, act_placed)
            full = jnp.dot(stack(h, act_placed, first), dec[...], preferred_element_type=F32)
            full = full.astype(BF16)
            for k in range(tile):
                part_send[h, first + k] = full[k * high:(k + 1) * high]

        tiles(go)
        part[h, 0] = part_send[h, 0]
        each(n - 1, lambda k: z_copy(PART, h, part_send, part, k + 1).start())

    for h in range(halves):
        encode(h)
        activate(h)
        decode(h)
        store(0, h, tok, tok_any).start()
        store(1, h, act_placed, act_any).start()

    bias = jnp.concatenate(
        [dbias[b:b + 1, :] for b in range(features // BLK)], axis=1
    )

    def rebuild(h):
        z_wait(PART, h, part)

        def go(j):
            _, c = source(j)

            def weight(o):
                other_bits, other = source(o)
                return wide(jnp.where((other_bits != 0) & (other == c), 1.0, 0.0).astype(F32))

            for at in range(0, high, 16):
                def add(o, total, at=at):
                    return total + weight(o) * part[h, o, at:at + 16, :].astype(F32)

                total = jnp.zeros((16, features), F32)
                if n <= 4:
                    for o in range(n):
                        total = add(o, total)
                else:
                    total = lax.fori_loop(0, n, add, total)
                wanted = goal[h, j, at:at + 16, :].astype(F32)
                err_send[h, j, at:at + 16, :] = (
                    ((total + bias) - wanted) * ERROR_SCALE
                ).astype(BF16)

        def send(k):
            go(k + 1)
            z_copy(ERR, h, err_send, err, k + 1).start()

        each(n - 1, send)
        go(0)
        err[h, 0] = err_send[h, 0]

    for h in range(halves):
        rebuild(h)

    def push_back(h):
        z_wait(ERR, h, err)

        def go(first):
            full = lax.dot_general(
                stack(h, err, first), dec[...], (((1,), (1,)), ((), ())),
                preferred_element_type=F32,
            )
            for k in range(tile):
                choose(h, first + k, full[k * high:(k + 1) * high], back_part)

        tiles(go)
        scatter(RS_BACK, h, back_part, back_in)

    def make_grad(h):
        scatter_wait(RS_BACK, h, back_in)

        def go(i):
            total = back_part[h, i, dp_rows(q), :].astype(F32)
            for j in range(1, n_dp):
                total = total + back_in[h, j, i].astype(F32)
            grad[h, i, dp_rows(q), :] = (total * slope[h, i]).astype(BF16)

        each(n, go)
        gather(AG_GRAD, h, grad)

    for h in range(halves):
        push_back(h)
        store(2, h, err, err_any).start()
        make_grad(h)

    for h in range(halves):
        gather_wait(AG_GRAD, h, grad)
        each(n, lambda i, h=h: place(h, i, grad, grad_placed))
        store(3, h, grad_placed, grad_any).start()

    each(n - 1, lambda k: c_copy(k + 1).wait_send())
    for h in range(halves):
        def settle_z(k, h=h):
            for phase, src, dst in (
                (TOK, tok_send, tok), (PART, part_send, part), (ERR, err_send, err)
            ):
                z_copy(phase, h, src, dst, k + 1).wait_send()

        def settle_d(k, h=h):
            for phase, src, dst in ((RS_PRE, pre_part, pre_in), (RS_BACK, back_part, back_in)):
                scatter_copy(phase, h, src, dst, k + 1).wait_send()
            for phase, buf in ((AG_ACT, act), (AG_GRAD, grad)):
                gather_copy(phase, h, buf, k + 1).wait_send()

        each(n - 1, settle_z)
        each(n_dp - 1, settle_d)
    for h in range(halves):
        for which, (src, dst) in enumerate((
            (tok, tok_any), (act_placed, act_any), (err, err_any), (grad_placed, grad_any)
        )):
            store(which, h, src, dst).wait()


def local(tokens, target, enc_weight, dec_weight, enc_bias, dec_bias, active, counts):
    n = lax.axis_size("latent")
    n_dp = lax.axis_size("dp")
    halves = max(1, BLK // (16 * n_dp))
    features = tokens.shape[1]
    own = enc_weight.shape[1]
    high = BLK // halves
    rows = high // n_dp
    vmem = pl.BlockSpec(memory_space=pltpu.VMEM)
    smem = pl.BlockSpec(memory_space=pltpu.SMEM)
    hbm = pl.BlockSpec(memory_space=pl.ANY)
    slots = pltpu.VMEM((halves, n, high, features), BF16)
    pairs = pltpu.VMEM((halves, n, high, MB * BLK), BF16)
    pieces = pltpu.VMEM((halves, n_dp, n, rows, MB * BLK), BF16)
    placed = pltpu.VMEM((halves, n, high, own), BF16)
    codes = pltpu.VMEM((n, 8, BLK), jnp.int32)
    dma = pltpu.SemaphoreType.DMA
    arrived = jax.ShapeDtypeStruct((halves, n, high, features), BF16)
    spread = jax.ShapeDtypeStruct((halves, n, high, own), BF16)
    rows_in, errors_in, acts, grads = pl.pallas_call(
        functools.partial(kernel, n, n_dp, halves),
        out_shape=(arrived, arrived, spread, spread),
        in_specs=[smem, vmem, hbm, hbm, hbm, hbm, vmem, vmem],
        out_specs=(hbm, hbm, hbm, hbm),
        scratch_shapes=[
            pltpu.VMEM(tokens.shape, BF16),
            pltpu.VMEM(target.shape, BF16),
            pltpu.VMEM(enc_weight.shape, BF16),
            pltpu.VMEM(dec_weight.shape, BF16),
            codes,
            codes,
            slots,
            slots,
            slots,
            slots,
            slots,
            slots,
            slots,
            pairs,
            pieces,
            pairs,
            pltpu.VMEM((halves, n, rows, MB * BLK), F32),
            pairs,
            pieces,
            pairs,
            placed,
            placed,
            dma((4,)),
            dma((4, halves)),
            dma((n,)),
            dma((n,)),
            dma((3, halves, n)),
            dma((3, halves, n)),
            dma((4, halves, n_dp)),
            dma((4, halves, n_dp)),
        ],
        compiler_params=pltpu.CompilerParams(
            collective_id=0, has_side_effects=True, vmem_limit_bytes=60 * 1024 * 1024
        ),
    )(
        counts, active, tokens, target, enc_weight, dec_weight,
        enc_bias.reshape(own // BLK, BLK), dec_bias.reshape(features // BLK, BLK),
    )
    depth = halves * n * high

    def transposed_dot(left, right):
        return lax.dot_general(
            left.reshape(depth, left.shape[-1]), right.reshape(depth, right.shape[-1]),
            (((0,), (0,)), ((), ())), preferred_element_type=F32,
        ).astype(BF16)

    return transposed_dot(rows_in, grads), transposed_dot(acts, errors_in)


def solution(mesh):
    placed = (
        P(("parts", "latent"), "dp"),
        P(("parts", "latent"), "dp"),
        P(("parts", "dp"), "latent"),
        P(("parts", "latent"), "dp"),
        P(("parts", "latent")),
        P(("parts", "dp")),
        P(("parts", "latent"), None),
        P(("parts", "latent")),
    )
    return jax.shard_map(
        local,
        mesh=mesh,
        in_specs=placed,
        out_specs=(P(("parts", "dp"), "latent"), P(("parts", "latent"), "dp")),
        check_vma=False,
    )
```

```python
import functools

import jax
import jax.numpy as jnp
from jax import lax
from jax.experimental import pallas as pl
from jax.experimental.pallas import tpu as pltpu
from jax.sharding import PartitionSpec as P

BLK = 128
MB = 2
ERROR_SCALE = 0.03125
GELU_C = 0.7978845608028654
GELU_A = 0.044715
TOK, PART, ERR = range(3)
RS_PRE, AG_ACT, RS_BACK, AG_GRAD = range(4)
F32 = jnp.float32
BF16 = jnp.bfloat16


def each(count, body):
    if count <= 4:
        for i in range(count):
            body(i)
    else:
        lax.fori_loop(0, count, lambda i, _: (body(i), None)[1], None)


def pair_masks(code, own_blocks):
    bits = code & 255
    rest = bits & (bits - 1)
    first = bits - rest
    return [
        [jnp.where(one == (1 << b), 1.0, 0.0).astype(F32) for b in range(own_blocks)]
        for one in (first, rest)
    ]


def kernel(
    n, n_dp, halves,
    counts, active, tokens_any, target_any, enc_any, dec_any, ebias, dbias,
    tok_any, err_any, act_any, grad_any,
    tokens, target, enc, dec, codes_out, codes_in,
    tok_send, goal, tok, part_send, part, err_send, err,
    pre_part, pre_in, act, slope, back_part, back_in, grad, act_placed, grad_placed,
    in_sem, out_sem, c_send, c_recv, z_send, z_recv, d_send, d_recv,
):
    me = lax.axis_index("latent")
    q = lax.axis_index("dp")
    high = BLK // halves
    rows = high // n_dp
    features = enc.shape[0]
    own_blocks = dec.shape[0] // BLK
    blocks, width = active.shape
    tile = min(n, 4)

    loads = [
        pltpu.make_async_copy(src, dst, in_sem.at[i])
        for i, (src, dst) in enumerate(
            ((tokens_any, tokens), (enc_any, enc), (dec_any, dec), (target_any, target))
        )
    ]
    for load in loads:
        load.start()

    barrier = pltpu.get_barrier_semaphore()

    def greet_z(j):
        pl.semaphore_signal(barrier, inc=1, device_id={"latent": lax.rem(me + j + 1, n)})

    def greet_d(j):
        pl.semaphore_signal(barrier, inc=1, device_id={"dp": lax.rem(q + j + 1, n_dp)})

    each(n - 1, greet_z)
    each(n_dp - 1, greet_d)

    row = lax.broadcasted_iota(jnp.int32, (blocks, width), 0)
    column = lax.broadcasted_iota(jnp.int32, (blocks, width), 1)
    used = jnp.zeros((blocks, width), jnp.int32)
    for t in range(blocks):
        used = jnp.where(row == t, counts[t], used)
    ids = active[...]
    place_bit = jnp.zeros((blocks, width), jnp.int32)
    for b in range(own_blocks):
        place_bit = jnp.where(ids % own_blocks == b, 1 << b, place_bit)
    value = (place_bit + 256 * row).astype(F32)
    owner = ids // own_blocks

    def encode_owner(k):
        total = jnp.where((column < used) & (owner == k), value, 0.0)
        total = jnp.sum(jnp.sum(total, axis=1, keepdims=True), axis=0, keepdims=True)
        codes_out[k] = jnp.broadcast_to(total, (8, BLK)).astype(jnp.int32)

    each(n, encode_owner)
    codes_in[0] = codes_out[me]

    def source(j):
        code = codes_out[lax.rem(me + j, n), 0:1, :]
        bits = code & 255
        total = code >> 8
        two = (bits & (bits - 1)) != 0
        return bits, jnp.where(two, total >> 1, total)

    def wide(mask):
        return jnp.concatenate([mask] * (features // BLK), axis=1)

    def chosen_rows(j, ref, at):
        _, c = source(j)
        total = None
        for t in range(blocks):
            weight = wide(jnp.where(c == t, 1.0, 0.0).astype(BF16))
            piece = weight * ref[t * BLK + at:t * BLK + at + 32, :]
            total = piece if total is None else total + piece
        return total

    def z_copy(phase, h, src, dst, j):
        return pltpu.make_async_remote_copy(
            src_ref=src.at[h, j],
            dst_ref=dst.at[h, n - j],
            send_sem=z_send.at[phase, h, j],
            recv_sem=z_recv.at[phase, h, n - j],
            device_id={"latent": lax.rem(me + j, n)},
        )

    def c_copy(j):
        return pltpu.make_async_remote_copy(
            src_ref=codes_out.at[lax.rem(me + j, n)],
            dst_ref=codes_in.at[n - j],
            send_sem=c_send.at[j],
            recv_sem=c_recv.at[n - j],
            device_id={"latent": lax.rem(me + j, n)},
        )

    def z_wait(phase, h, ref):
        each(n - 1, lambda k: pltpu.make_async_remote_copy(
            src_ref=ref.at[h, k + 1],
            dst_ref=ref.at[h, k + 1],
            send_sem=z_send.at[phase, h, k + 1],
            recv_sem=z_recv.at[phase, h, k + 1],
            device_id={"latent": lax.rem(me + k + 1, n)},
        ).wait_recv())

    def c_wait(j):
        pltpu.make_async_remote_copy(
            src_ref=codes_in.at[j],
            dst_ref=codes_in.at[j],
            send_sem=c_send.at[j],
            recv_sem=c_recv.at[j],
            device_id={"latent": lax.rem(me + j, n)},
        ).wait_recv()

    def d_copy(phase, h, src, dst, j):
        return pltpu.make_async_remote_copy(
            src_ref=src,
            dst_ref=dst,
            send_sem=d_send.at[phase, h, j],
            recv_sem=d_recv.at[phase, h, n_dp - j],
            device_id={"dp": lax.rem(q + j, n_dp)},
        )

    def d_wait(phase, h, ref, j):
        pltpu.make_async_remote_copy(
            src_ref=ref,
            dst_ref=ref,
            send_sem=d_send.at[phase, h, j],
            recv_sem=d_recv.at[phase, h, j],
            device_id={"dp": lax.rem(q + j, n_dp)},
        ).wait_recv()

    every = pl.ds(0, n)

    def dp_rows(p):
        return pl.ds(pl.multiple_of(p * rows, rows), rows)

    def scatter_copy(phase, h, src, dst, j):
        peer = lax.rem(q + j, n_dp)
        return d_copy(phase, h, src.at[h, every, dp_rows(peer)], dst.at[h, n_dp - j], j)

    def scatter(phase, h, src, dst):
        each(n_dp - 1, lambda k: scatter_copy(phase, h, src, dst, k + 1).start())

    def scatter_wait(phase, h, dst):
        each(n_dp - 1, lambda k: d_wait(phase, h, dst.at[h, k + 1], k + 1))

    def gather_copy(phase, h, buf, j):
        mine = buf.at[h, every, dp_rows(q)]
        return d_copy(phase, h, mine, mine, j)

    def gather(phase, h, buf):
        each(n_dp - 1, lambda k: gather_copy(phase, h, buf, k + 1).start())

    def gather_wait(phase, h, buf):
        each(n_dp - 1, lambda k: d_wait(
            phase, h, buf.at[h, every, dp_rows(lax.rem(q + k + 1, n_dp))], k + 1
        ))

    loads[0].wait()
    for h in range(halves):
        def stage(j, h=h):
            for at in range(0, high, 32):
                tok_send[h, j, at:at + 32, :] = chosen_rows(j, tokens, h * high + at)

        each(n - 1, lambda k: stage(k + 1))
        if h == 0:
            pl.semaphore_wait(barrier, n - 1 + n_dp - 1)
            each(n - 1, lambda k: c_copy(k + 1).start())
        if h > 0:
            each(n - 1, lambda k, h=h: z_copy(TOK, h - 1, tok_send, tok, k + 1).wait_send())
        each(n - 1, lambda k, h=h: z_copy(TOK, h, tok_send, tok, k + 1).start())
    for h in range(halves):
        for at in range(0, high, 32):
            tok[h, 0, at:at + 32, :] = chosen_rows(0, tokens, h * high + at)
    loads[3].wait()

    def aim(j):
        for h in range(halves):
            for at in range(0, high, 32):
                goal[h, j, at:at + 32, :] = chosen_rows(j, target, h * high + at)

    each(n, aim)
    loads[1].wait()
    each(n - 1, lambda k: c_wait(k + 1))
    loads[2].wait()

    def store(which, h, src, dst):
        return pltpu.make_async_copy(src.at[h], dst.at[h], out_sem.at[which, h])

    def masks_of(i):
        return pair_masks(codes_in[i, 0:1, :], own_blocks)

    def tiles(body):
        each(n // tile, lambda k: body(k * tile))

    def stack(h, buf, first):
        block = buf[h, pl.ds(first, tile)]
        return block.reshape(tile * high, block.shape[-1])

    def choose(h, i, full, dst):
        for r, mask in enumerate(masks_of(i)):
            total = mask[0] * full[:, :BLK]
            for b in range(1, own_blocks):
                total = total + mask[b] * full[:, b * BLK:(b + 1) * BLK]
            dst[h, i, :, r * BLK:(r + 1) * BLK] = total.astype(BF16)

    def place(h, i, src, dst):
        low, rest = masks_of(i)
        first = src[h, i, :, :BLK].astype(F32)
        second = src[h, i, :, BLK:].astype(F32)
        for b in range(own_blocks):
            dst[h, i, :, b * BLK:(b + 1) * BLK] = (
                low[b] * first + rest[b] * second
            ).astype(BF16)

    def encode(h):
        z_wait(TOK, h, tok)

        def go(first):
            full = jnp.dot(stack(h, tok, first), enc[...], preferred_element_type=F32)
            for k in range(tile):
                choose(h, first + k, full[k * high:(k + 1) * high], pre_part)

        tiles(go)
        scatter(RS_PRE, h, pre_part, pre_in)

    def activate(h):
        scatter_wait(RS_PRE, h, pre_in)

        def go(i):
            total = pre_part[h, i, dp_rows(q), :].astype(F32)
            for j in range(1, n_dp):
                total = total + pre_in[h, j, i].astype(F32)
            for r, mask in enumerate(masks_of(i)):
                live = sum(mask)
                bias = sum(mask[b] * ebias[b:b + 1, :] for b in range(own_blocks))
                v = total[:, r * BLK:(r + 1) * BLK] + bias
                t = jnp.tanh(GELU_C * (v + GELU_A * (v * v * v)))
                a = 0.5 * v * (1.0 + t)
                s = 0.5 * (1.0 + t) + 0.5 * v * (1.0 - t * t) * (
                    GELU_C * (1.0 + 3.0 * GELU_A * (v * v))
                )
                act[h, i, dp_rows(q), r * BLK:(r + 1) * BLK] = (a * live).astype(BF16)
                slope[h, i, :, r * BLK:(r + 1) * BLK] = s * live

        each(n, go)
        gather(AG_ACT, h, act)

    def decode(h):
        gather_wait(AG_ACT, h, act)

        def go(first):
            for k in range(tile):
                place(h, first + k, act, act_placed)
            full = jnp.dot(stack(h, act_placed, first), dec[...], preferred_element_type=F32)
            full = full.astype(BF16)
            for k in range(tile):
                part_send[h, first + k] = full[k * high:(k + 1) * high]

        tiles(go)
        part[h, 0] = part_send[h, 0]
        each(n - 1, lambda k: z_copy(PART, h, part_send, part, k + 1).start())

    for h in range(halves):
        encode(h)
        activate(h)
        decode(h)
        store(0, h, tok, tok_any).start()
        store(1, h, act_placed, act_any).start()

    bias = jnp.concatenate(
        [dbias[b:b + 1, :] for b in range(features // BLK)], axis=1
    )

    def rebuild(h):
        z_wait(PART, h, part)

        def go(j):
            _, c = source(j)

            def weight(o):
                other_bits, other = source(o)
                return wide(jnp.where((other_bits != 0) & (other == c), 1.0, 0.0).astype(F32))

            for at in range(0, high, 16):
                def add(o, total, at=at):
                    return total + weight(o) * part[h, o, at:at + 16, :].astype(F32)

                total = jnp.zeros((16, features), F32)
                if n <= 4:
                    for o in range(n):
                        total = add(o, total)
                else:
                    total = lax.fori_loop(0, n, add, total)
                wanted = goal[h, j, at:at + 16, :].astype(F32)
                err_send[h, j, at:at + 16, :] = (
                    ((total + bias) - wanted) * ERROR_SCALE
                ).astype(BF16)

        def send(k):
            go(k + 1)
            z_copy(ERR, h, err_send, err, k + 1).start()

        each(n - 1, send)
        go(0)
        err[h, 0] = err_send[h, 0]

    for h in range(halves):
        rebuild(h)

    def push_back(h):
        z_wait(ERR, h, err)

        def go(first):
            full = lax.dot_general(
                stack(h, err, first), dec[...], (((1,), (1,)), ((), ())),
                preferred_element_type=F32,
            )
            for k in range(tile):
                choose(h, first + k, full[k * high:(k + 1) * high], back_part)

        tiles(go)
        scatter(RS_BACK, h, back_part, back_in)

    def make_grad(h):
        scatter_wait(RS_BACK, h, back_in)

        def go(i):
            total = back_part[h, i, dp_rows(q), :].astype(F32)
            for j in range(1, n_dp):
                total = total + back_in[h, j, i].astype(F32)
            grad[h, i, dp_rows(q), :] = (total * slope[h, i]).astype(BF16)

        each(n, go)
        gather(AG_GRAD, h, grad)

    for h in range(halves):
        push_back(h)
        store(2, h, err, err_any).start()
        make_grad(h)

    for h in range(halves):
        gather_wait(AG_GRAD, h, grad)
        each(n, lambda i, h=h: place(h, i, grad, grad_placed))
        store(3, h, grad_placed, grad_any).start()

    each(n - 1, lambda k: c_copy(k + 1).wait_send())
    for h in range(halves):
        def settle_z(k, h=h):
            for phase, src, dst in (
                (TOK, tok_send, tok), (PART, part_send, part), (ERR, err_send, err)
            ):
                if phase != TOK or h == halves - 1:
                    z_copy(phase, h, src, dst, k + 1).wait_send()

        def settle_d(k, h=h):
            for phase, src, dst in ((RS_PRE, pre_part, pre_in), (RS_BACK, back_part, back_in)):
                scatter_copy(phase, h, src, dst, k + 1).wait_send()
            for phase, buf in ((AG_ACT, act), (AG_GRAD, grad)):
                gather_copy(phase, h, buf, k + 1).wait_send()

        each(n - 1, settle_z)
        each(n_dp - 1, settle_d)
    for h in range(halves):
        for which, (src, dst) in enumerate((
            (tok, tok_any), (act_placed, act_any), (err, err_any), (grad_placed, grad_any)
        )):
            store(which, h, src, dst).wait()


def local(tokens, target, enc_weight, dec_weight, enc_bias, dec_bias, active, counts):
    n = lax.axis_size("latent")
    n_dp = lax.axis_size("dp")
    halves = max(1, BLK // (16 * n_dp))
    features = tokens.shape[1]
    own = enc_weight.shape[1]
    high = BLK // halves
    rows = high // n_dp
    vmem = pl.BlockSpec(memory_space=pltpu.VMEM)
    smem = pl.BlockSpec(memory_space=pltpu.SMEM)
    hbm = pl.BlockSpec(memory_space=pl.ANY)
    slots = pltpu.VMEM((halves, n, high, features), BF16)
    pairs = pltpu.VMEM((halves, n, high, MB * BLK), BF16)
    pieces = pltpu.VMEM((halves, n_dp, n, rows, MB * BLK), BF16)
    placed = pltpu.VMEM((halves, n, high, own), BF16)
    codes = pltpu.VMEM((n, 8, BLK), jnp.int32)
    dma = pltpu.SemaphoreType.DMA
    arrived = jax.ShapeDtypeStruct((halves, n, high, features), BF16)
    spread = jax.ShapeDtypeStruct((halves, n, high, own), BF16)
    rows_in, errors_in, acts, grads = pl.pallas_call(
        functools.partial(kernel, n, n_dp, halves),
        out_shape=(arrived, arrived, spread, spread),
        in_specs=[smem, vmem, hbm, hbm, hbm, hbm, vmem, vmem],
        out_specs=(hbm, hbm, hbm, hbm),
        scratch_shapes=[
            pltpu.VMEM(tokens.shape, BF16),
            pltpu.VMEM(target.shape, BF16),
            pltpu.VMEM(enc_weight.shape, BF16),
            pltpu.VMEM(dec_weight.shape, BF16),
            codes,
            codes,
            slots,
            slots,
            slots,
            slots,
            slots,
            slots,
            slots,
            pairs,
            pieces,
            pairs,
            pltpu.VMEM((halves, n, rows, MB * BLK), F32),
            pairs,
            pieces,
            pairs,
            placed,
            placed,
            dma((4,)),
            dma((4, halves)),
            dma((n,)),
            dma((n,)),
            dma((3, halves, n)),
            dma((3, halves, n)),
            dma((4, halves, n_dp)),
            dma((4, halves, n_dp)),
        ],
        compiler_params=pltpu.CompilerParams(
            collective_id=0, has_side_effects=True, vmem_limit_bytes=60 * 1024 * 1024
        ),
    )(
        counts, active, tokens, target, enc_weight, dec_weight,
        enc_bias.reshape(own // BLK, BLK), dec_bias.reshape(features // BLK, BLK),
    )
    depth = halves * n * high

    def transposed_dot(left, right):
        return lax.dot_general(
            left.reshape(depth, left.shape[-1]), right.reshape(depth, right.shape[-1]),
            (((0,), (0,)), ((), ())), preferred_element_type=F32,
        ).astype(BF16)

    return transposed_dot(rows_in, grads), transposed_dot(acts, errors_in)


def solution(mesh):
    placed = (
        P(("parts", "latent"), "dp"),
        P(("parts", "latent"), "dp"),
        P(("parts", "dp"), "latent"),
        P(("parts", "latent"), "dp"),
        P(("parts", "latent")),
        P(("parts", "dp")),
        P(("parts", "latent"), None),
        P(("parts", "latent")),
    )
    return jax.shard_map(
        local,
        mesh=mesh,
        in_specs=placed,
        out_specs=(P(("parts", "dp"), "latent"), P(("parts", "latent"), "dp")),
        check_vma=False,
    )
```
